32 devices in a mesh: groups: 2 (over y), expert: 16 (over z, x, core).
Axes of the slice: x: 2, y: 2, z: 4, core: 2. Of those that a mesh axis runs over, the one named last changes fastest.
Arguments:
- tokens: bfloat16 [4096, 1024], P(('groups', 'expert')), parts along dimension 0, may hold values from -6 to 6
- segments: int32 [32, 128], P(('groups', 'expert')), parts along dimension 0, may hold values from 0 to 3, never falling along the last dimension, each value on 1 to 64 neighbouring positions
- lengths: int32 [32], P(('groups', 'expert')), parts along dimension 0, may hold values from 32 to 128
- attn_gain: float32 [1024], replicated, may hold values from 0.1 to 1.9
- attn_weight: bfloat16 [1024, 4096], P(None, 'expert'), may hold values from -0.1875 to 0.1875
- ffn_gain: float32 [1024], replicated, may hold values from 0.1 to 1.9
- routes: int32 [4096, 2], P(('groups', 'expert')), parts along dimension 0, may hold values from 0 to 7, all different within a row; in each aligned block of 128 rows (0 to 127, 128 to 255, ...) at most 40 rows name the same one
- route_gates: float32 [4096, 2], P(('groups', 'expert')), parts along dimension 0, may hold values from 0.2 to 1
- expert_in: bfloat16 [16, 1024, 2048], P('expert'), may hold values from -0.1875 to 0.1875
- expert_out: bfloat16 [16, 2048, 1024], P('expert'), may hold values from -0.09375 to 0.09375
- teacher: float32 [32, 4, 1024], P(('groups', 'expert')), parts along dimension 0, may hold values from -6 to 6
Outputs:
- grad_tokens: bfloat16 [4096, 1024], P(('groups', 'expert')), parts along dimension 0
- pooled: float32 [32, 4, 1024], P(('groups', 'expert')), parts along dimension 0
The draws below stay inside these ranges and needn't reach their ends.
There are 2 independent parts, one for each index of `groups`. The reference program is written for one: setup_inputs(seed, part) draws one part's arguments, and reference() takes and returns one part's arrays. A program takes and returns all parts, laid end to end along the dimension named above; an argument that names none is the same for every part. Nothing has to cross between parts.
Inputs may be any that keep to these rules, and one draw needn't show every extreme that they name: `routes`: each token names two different experts; among the 128 tokens of one device no expert is named more than 40 times. `segments`: within a row segment numbers never fall, and each of the 4 sentences holds 1 to 64 positions.
All inputs are finite; a program needn't handle non-finite values.
Results may differ from the reference program's by a relative error of at most 0.029.
The reference program's roundings to bfloat16 on the way count: a program that leaves them out, or rounds other values in their place, can miss the bound.
Values may be sent and summed in bfloat16 or wider, within the bound.
A program may use at most 128 MiB of HBM per device.

```python
import math
import jax
import jax.numpy as jnp
import numpy as np
from jax import lax

D = 1024
HEADS = 8
FF = 4096
SPLIT = 2
EXPERTS = 8
FF_DEV = 2048
LEN = 128
SEG_ROW = 4
SEG_MOST = 64
TOK_DEV = 128
ROWS = 16
TOKENS = 2048
CAP = 40
N_EXPERT = 16


def plant(drawn, rng, smallest, top_value):
    longest = drawn.shape.index(max(drawn.shape))
    spots = []
    for shift in (0, 1):
        where = [jax.random.randint(jax.random.fold_in(rng, axis), (), 0, length) for axis, length in enumerate(drawn.shape)]
        where[longest] = (where[longest] + shift) % drawn.shape[longest]
        spots.append(tuple(where))
    return drawn.at[spots[0]].set(smallest).at[spots[1]].set(top_value)


def block_scale(key, extent, cuts, least, largest):
    level = 1.0
    for dim, parts in cuts:
        steps = jax.random.uniform(jax.random.fold_in(jax.random.fold_in(key, 6), dim), (parts,), jnp.float32, least / len(cuts), largest / len(cuts))
        level = level * jnp.repeat(jnp.exp(steps), extent[dim] // parts).reshape((-1,) + (1,) * (len(extent) - 1 - dim))
    return level


def split_up(number_of, total, most, skew):
    weights = [(1 << 20) // math.isqrt(standing ** skew) + 1 for standing in range(2, number_of + 1)]
    rest, given = total - most - (number_of - 1), [1] * (number_of - 1)
    while rest > 0:
        movable = [i for i in range(number_of - 1) if given[i] < most]
        mass, budget = sum([weights[i] for i in movable]), rest
        for i in movable:
            more = min(most - given[i], max(1, budget * weights[i] // mass), rest)
            given[i] = given[i] + more
            rest = rest - more
    return np.array([most] + given)


def ragged(own_key, count, total, limit, skew):
    if count == 2:
        one = jax.random.randint(own_key, (), max(1, total - limit), min(limit, total - 1) + 1)
        return jnp.stack([one, total - one])
    sizes = jnp.asarray(split_up(count, total, limit, skew), jnp.int32)
    couples = (count - 1) // 2
    source_of, taker = sizes[1:1 + 2 * couples:2], sizes[2:2 + 2 * couples:2]
    slack = jnp.minimum(source_of - 1, limit - taker)
    shifted = jax.random.randint(jax.random.fold_in(own_key, 1), (couples,), 0, 1 << 20) % (slack + 1)
    sizes = sizes.at[1:1 + 2 * couples:2].set(source_of - shifted).at[2:2 + 2 * couples:2].set(taker + shifted)
    return sizes[jax.random.permutation(jax.random.fold_in(own_key, 2), count)]


def routed_block(key, own, number, rows, amount, top, bound, lean):
    sequence = jax.random.permutation(key, amount)
    crowded, ordinary = portions_of(amount, rows * top, bound, lean, True), portions_of(amount, rows * top, bound, lean, False)
    places = jnp.arange(amount)

    def named(tallies, turn):
        used = int((tallies > 0).sum())
        fixed = max(1, used // 4)
        moved = fixed + (places - fixed + turn * (used - fixed)) % max(1, amount - fixed)
        return jnp.zeros((amount,), jnp.int32).at[sequence[jnp.where(places < fixed, places, moved)]].set(jnp.asarray(tallies, jnp.int32))

    tallies = jnp.where(number % 4 == 0, named(crowded, number // 4), named(ordinary, number - number // 4 - 1))
    mixed = jax.random.permutation(jax.random.fold_in(own, 3), amount)
    giver, taker = mixed[0:amount // 2 * 2:2], mixed[1:amount // 2 * 2:2]
    slack = jnp.minimum(tallies[giver] - 1, bound - tallies[taker]) // 2
    slack = jnp.where((giver == sequence[0]) | (taker == sequence[0]) | (tallies[taker] == 0), 0, jnp.maximum(slack, 0))
    moved = jax.random.randint(jax.random.fold_in(own, 4), (amount // 2,), 0, 1 << 20) % (slack + 1)
    tallies = tallies.at[giver].add(-moved).at[taker].add(moved)
    labels = jnp.searchsorted(jnp.cumsum(tallies), jnp.arange(rows * top), side="right").astype(jnp.int32)
    table = labels.reshape(top, rows).T
    table = table[jax.random.permutation(jax.random.fold_in(own, 1), rows)]
    turn = jax.random.randint(jax.random.fold_in(own, 2), (rows, 1), 0, top)
    return jnp.take_along_axis(table, (jnp.arange(top)[None, :] + turn) % top, axis=1)


def portions_of(count, total, bound, slope, full):
    weights = [(1 << 20) // math.isqrt(rank ** slope) + 1 for rank in range(1, count + 1)]
    largest = bound if full else min(bound, max(-(-total // count), total * weights[0] // sum(weights)))
    least = 1 if total - largest >= count - 1 else 0
    given, rest = [largest] + [least] * (count - 1), total - largest - least * (count - 1)
    while rest > 0:
        candidates = [i for i in range(1, count) if given[i] < largest] or [i for i in range(1, count) if given[i] < bound]
        mass, budget = sum([weights[i] for i in candidates]), rest
        for i in candidates:
            extra = min(bound - given[i], max(1, budget * weights[i] // mass), rest)
            given[i] = given[i] + extra
            rest = rest - extra
    return np.array(given)


def noise(stream_key, shape, deviation, most, cuts=(), kind=jnp.bfloat16):
    result = jax.random.normal(stream_key, shape, jnp.float32) * deviation
    if len(cuts) > 0:
        result = block_scale(stream_key, shape, cuts, -0.22, 0.18) * result
    return jnp.clip(result, min=-most, max=most).astype(kind)


def setup_inputs(seed: int = 0, part: int = 0) -> dict:
    seeds = jax.random.split(jax.random.key(seed), 12)
    part_keys = jax.random.split(jax.random.fold_in(seeds[11], part), 12)
    tokens = noise(part_keys[0], (TOKENS, D), 1.0, 6.0, ((0, 16),))
    segments = jax.vmap(lambda own: jnp.searchsorted(jnp.cumsum(ragged(own, SEG_ROW, LEN, SEG_MOST, 1)), jnp.arange(LEN), side="right"))(jax.random.split(part_keys[1], ROWS)).reshape((ROWS, LEN)).astype(jnp.int32)
    lengths = plant(jax.random.randint(part_keys[2], (ROWS,), LEN // 4, LEN + 1), jax.random.fold_in(part_keys[2], 1), LEN // 4, LEN).astype(jnp.int32)
    attn_gain = jnp.clip(1.0 + 0.18 * jax.random.normal(seeds[3], (D,), jnp.float32), 0.1, 1.9)
    attn_weight = noise(seeds[4], (D, 4 * D), D ** -0.5, 0.1875, ((1, 16),))
    ffn_gain = jnp.clip(1.0 + 0.18 * jax.random.normal(seeds[5], (D,), jnp.float32), 0.1, 1.9)
    routes_keys = jax.random.split(jax.random.fold_in(part_keys[6], 1), TOKENS // TOK_DEV)
    routes_turns = jax.random.permutation(jax.random.fold_in(part_keys[6], 3), TOKENS // TOK_DEV)
    routes = jax.vmap(lambda own, number: routed_block(jax.random.fold_in(part_keys[6], 2), own, number, TOK_DEV, EXPERTS, 2, CAP, 2))(routes_keys, routes_turns).reshape((TOKENS, 2))
    route_gates = jnp.clip(0.2 + 0.8 * jax.random.uniform(part_keys[7], (TOKENS, 2), jnp.float32) ** block_scale(part_keys[7], (TOKENS, 2), ((0, 16),), -0.2, 0.2), 0.2, 1.0)
    expert_in = noise(seeds[8], (EXPERTS * SPLIT, D, FF_DEV), D ** -0.5, 0.1875, ((0, 16),))
    expert_out = noise(seeds[9], (EXPERTS * SPLIT, FF_DEV, D), FF ** -0.5, 0.09375, ((0, 16),))
    teacher = noise(part_keys[10], (ROWS, SEG_ROW, D), 1.0, 6.0, ((0, 16),), jnp.float32)
    return dict(tokens=tokens, segments=segments, lengths=lengths, attn_gain=attn_gain, attn_weight=attn_weight, ffn_gain=ffn_gain, routes=routes, route_gates=route_gates, expert_in=expert_in, expert_out=expert_out, teacher=teacher)


epsilon = 1e-05

def layer_norm(inputs, scale_gain):
    average = lax.optimization_barrier(jnp.mean(inputs, axis=-1, keepdims=True))
    centred = inputs - average
    variance = lax.optimization_barrier(jnp.mean(centred * centred, axis=-1, keepdims=True))
    return centred * lax.rsqrt(variance + epsilon) * scale_gain

def key_allowed(segments, lengths):
    positions = jnp.arange(segments.shape[1], dtype=jnp.int32)
    same_seg = segments[:, :, None] == segments[:, None, :]
    key_live = positions[None, None, :] < lengths[:, None, None]
    itself = positions[:, None] == positions[None, :]
    return jnp.logical_or(jnp.logical_and(same_seg, key_live), itself[None])

def attend(inputs, weight, allowed, scale_gain, head_count):
    row_count, length, model_width = inputs.shape
    head_width = model_width // head_count
    normed = layer_norm(inputs, scale_gain).astype(jnp.bfloat16).reshape(row_count * length, model_width)
    projected = jnp.dot(normed, weight[:, :3 * model_width], preferred_element_type=jnp.float32).astype(jnp.bfloat16)
    projected = projected.reshape(row_count, length, 3, head_count, head_width)
    queries = projected[:, :, 0].astype(jnp.float32)
    keys_all = projected[:, :, 1].astype(jnp.float32)
    values_all = projected[:, :, 2].astype(jnp.float32)
    scores = jnp.einsum('rqhd,rkhd->rhqk', queries, keys_all) * head_width ** (-0.5)
    weights_exp = jnp.exp(scores) * allowed[:, None].astype(jnp.float32)
    probabilities = (weights_exp / lax.optimization_barrier(jnp.sum(weights_exp, axis=-1, keepdims=True))).astype(jnp.bfloat16)
    context = jnp.einsum('rhqk,rkhd->rqhd', probabilities.astype(jnp.float32), values_all).astype(jnp.bfloat16)
    context = context.reshape(row_count * length, model_width)
    output = jnp.dot(context, weight[:, 3 * model_width:], preferred_element_type=jnp.float32)
    return inputs + output.reshape(row_count, length, model_width)

def slot_places(block_routes, experts, capacity):
    flat_ids = block_routes.reshape(-1).astype(jnp.int32)
    onehot = (flat_ids[:, None] == jnp.arange(experts, dtype=jnp.int32)[None, :]).astype(jnp.int32)
    earlier = jnp.cumsum(onehot, axis=0, dtype=jnp.int32) - onehot
    position = lax.optimization_barrier(jnp.sum(earlier * onehot, axis=1, dtype=jnp.int32))
    return (flat_ids * capacity + position).astype(jnp.int32)

def reference(tokens, segments, lengths, attn_gain, attn_weight, ffn_gain, routes, route_gates, expert_in, expert_out, teacher):
    devices = N_EXPERT
    experts = EXPERTS
    capacity = CAP
    allowed = key_allowed(segments, lengths)
    inputs = tokens.astype(jnp.float32).reshape(ROWS, LEN, D)

    def attention_part(source):
        return attend(source, attn_weight, allowed, attn_gain, HEADS)
    hidden_state, attn_pull = jax.vjp(attention_part, inputs)
    hidden_flat = hidden_state.reshape(TOKENS, D)

    def ffn_norm(source):
        return layer_norm(source, ffn_gain)
    normed_ffn, norm_pull = jax.vjp(ffn_norm, hidden_flat)
    normed_bf = normed_ffn.astype(jnp.bfloat16)
    slot_place = jax.vmap(lambda block_routes: slot_places(block_routes, experts, capacity))(routes.reshape(devices, TOK_DEV, 2))

    def fill_slots(place_block, rows_block):
        return jnp.zeros((experts * capacity, D), rows_block.dtype).at[place_block].set(rows_block)

    def to_experts(per_device):
        return per_device.reshape(devices, experts, capacity, D).transpose(1, 0, 2, 3).reshape(experts, devices * capacity, D)

    def from_experts(per_expert):
        return per_expert.reshape(experts, devices, capacity, D).transpose(1, 0, 2, 3).reshape(devices, experts * capacity, D)

    def pick_slots(table_rows, slot_index):
        return jnp.take(table_rows, slot_index, axis=0)
    rows_rep = jnp.repeat(normed_bf.reshape(devices, TOK_DEV, D), 2, axis=1)
    per_expert = to_experts(jax.vmap(fill_slots)(slot_place, rows_rep))
    weight_in_all = expert_in.reshape(experts, SPLIT, D, FF_DEV)
    weight_out_all = expert_out.reshape(experts, SPLIT, FF_DEV, D)

    def expert_forward(operands):
        expert_rows, weight_in, weight_out = operands
        summed = jnp.zeros((expert_rows.shape[0], D), jnp.float32)
        hiddens = []
        for half_index in range(SPLIT):
            hidden = jnp.maximum(jnp.dot(expert_rows, weight_in[half_index], preferred_element_type=jnp.float32), 0.0).astype(jnp.bfloat16)
            partial_out = jnp.dot(hidden, weight_out[half_index], preferred_element_type=jnp.float32).astype(jnp.bfloat16)
            summed = summed + partial_out.astype(jnp.float32)
            hiddens.append(hidden)
        return (summed, jnp.stack(hiddens))
    totals, hiddens_all = lax.map(expert_forward, (per_expert, weight_in_all, weight_out_all))
    picked = jax.vmap(pick_slots)(from_experts(totals), slot_place)
    expert_sum = lax.optimization_barrier(jnp.sum(picked.reshape(TOKENS, 2, D) * route_gates[:, :, None], axis=1))
    outputs = hidden_flat + expert_sum
    positions = jnp.arange(LEN, dtype=jnp.int32)
    live_mask = positions[None, :] < lengths[:, None]
    member_int = jnp.logical_and(segments[:, :, None] == jnp.arange(SEG_ROW, dtype=jnp.int32)[None, None, :], live_mask[:, :, None]).astype(jnp.int32)
    member = member_int.astype(jnp.float32)
    counts = lax.optimization_barrier(jnp.sum(member_int, axis=1, dtype=jnp.int32))
    pooled = jnp.einsum('rls,rld->rsd', member, outputs.reshape(ROWS, LEN, D), precision=lax.Precision.HIGHEST)
    pooled = pooled / jnp.maximum(counts, 1).astype(jnp.float32)[:, :, None]
    difference = pooled - teacher
    grad_out = jnp.einsum('rls,rsd->rld', member, difference, precision=lax.Precision.HIGHEST).reshape(TOKENS, D)
    slot_grads = (grad_out[:, None, :] * route_gates[:, :, None]).astype(jnp.bfloat16).reshape(devices, 2 * TOK_DEV, D)
    per_expert_grads = to_experts(jax.vmap(fill_slots)(slot_place, slot_grads))
    contract = (((1,), (1,)), ((), ()))

    def expert_backward(operands):
        expert_grads, hiddens, weight_in, weight_out = operands
        summed = jnp.zeros((expert_grads.shape[0], D), jnp.float32)
        for half_index in range(SPLIT):
            product = lax.dot_general(expert_grads, weight_out[half_index], contract, preferred_element_type=jnp.float32)
            grad_pre = jnp.where(hiddens[half_index] > 0, product, 0.0).astype(jnp.bfloat16)
            grad_part = lax.dot_general(grad_pre, weight_in[half_index], contract, preferred_element_type=jnp.float32).astype(jnp.bfloat16)
            summed = summed + grad_part.astype(jnp.float32)
        return summed
    grad_totals = lax.map(expert_backward, (per_expert_grads, hiddens_all, weight_in_all, weight_out_all))
    grad_picked = jax.vmap(pick_slots)(from_experts(grad_totals), slot_place)
    grad_normed = lax.optimization_barrier(jnp.sum(grad_picked.reshape(TOKENS, 2, D), axis=1))
    grad_hidden = grad_out + norm_pull(grad_normed)[0]
    grad_inputs = attn_pull(grad_hidden.reshape(ROWS, LEN, D))[0]
    grad_tokens = grad_inputs.reshape(TOKENS, D).astype(jnp.bfloat16)
    return (grad_tokens, pooled)
```

```python
import functools

import jax
import jax.numpy as jnp
from jax import lax
from jax.experimental import pallas as pl
from jax.experimental.pallas import tpu as pltpu
from jax.sharding import PartitionSpec as P

HEADS = 8
SPLIT = 2
MESH = pl.DeviceIdType.MESH
NT = (((1,), (1,)), ((), ()))
TILE = 256


epsilon = 1e-05


def layer_norm(inputs, scale_gain):
    average = jnp.mean(inputs, axis=-1, keepdims=True)
    centred = inputs - average
    variance = jnp.mean(centred * centred, axis=-1, keepdims=True)
    return centred * lax.rsqrt(variance + epsilon) * scale_gain


def key_allowed(segments, lengths):
    positions = jnp.arange(segments.shape[1], dtype=jnp.int32)
    same_seg = segments[:, :, None] == segments[:, None, :]
    key_live = positions[None, None, :] < lengths[:, None, None]
    itself = positions[:, None] == positions[None, :]
    return jnp.logical_or(jnp.logical_and(same_seg, key_live), itself[None])


def attend(inputs, weight, allowed, scale_gain, head_count):
    row_count, length, model_width = inputs.shape
    head_width = model_width // head_count
    normed = (
        layer_norm(inputs, scale_gain).astype(jnp.bfloat16).reshape(row_count * length, model_width)
    )
    projected = jnp.dot(
        normed, weight[:, : 3 * model_width], preferred_element_type=jnp.float32
    ).astype(jnp.bfloat16)
    projected = projected.reshape(row_count, length, 3, head_count, head_width)
    queries = projected[:, :, 0]
    keys_all = projected[:, :, 1]
    values_all = projected[:, :, 2]
    scores = jnp.einsum(
        "rqhd,rkhd->rhqk", queries, keys_all, preferred_element_type=jnp.float32
    ) * head_width ** (-0.5)
    weights_exp = jnp.exp(scores) * allowed[:, None].astype(jnp.float32)
    probabilities = (weights_exp / jnp.sum(weights_exp, axis=-1, keepdims=True)).astype(
        jnp.bfloat16
    )
    context = jnp.einsum(
        "rhqk,rkhd->rqhd", probabilities, values_all, preferred_element_type=jnp.float32
    ).astype(jnp.bfloat16)
    context = context.reshape(row_count * length, model_width)
    output = jnp.dot(context, weight[:, 3 * model_width :], preferred_element_type=jnp.float32)
    return inputs + output.reshape(row_count, length, model_width)


def flip(index, bits, count):
    result, place = 0, 1
    while place < count:
        bit = lax.rem(lax.div(index, place), 2)
        if (bits // place) % 2:
            bit = 1 - bit
        result = result + bit * place
        place *= 2
    return result


def unfold(block):
    wide = block.astype(jnp.float32)
    cap = wide.shape[0] // 2
    return jnp.concatenate([wide[:cap], wide[cap:]], axis=1)


def fold(rows):
    half = rows.shape[1] // 2
    return jnp.concatenate([rows[:, :half], rows[:, half:]], axis=0)


def expert_kernel(chips, backward, groups_of, *refs):
    if backward:
        packed, w1_hbm, w2_hbm, kept, out = refs[:5]
        rest = refs[5:]
    else:
        packed, w1_hbm, w2_hbm, out, kept = refs[:5]
        rest = refs[5:]
    (w1, w2, got_a, got_b, x_ref, h_scr, part, to_pair, from_pair, to_back,
     w_sem, send_a, recv_a, send_b, recv_b, send_c, recv_c, send_d, recv_d) = rest
    rank = lax.axis_index("expert")
    core = lax.rem(rank, 2)
    chip = lax.div(rank, 2)
    pair = 2 * chip + (1 - core)
    cap = packed.shape[1] // 2
    load_1 = pltpu.make_async_copy(w1_hbm.at[0], w1, w_sem.at[0])
    load_2 = pltpu.make_async_copy(w2_hbm.at[0], w2, w_sem.at[1])
    load_1.start()
    load_2.start()
    peer_chip = [flip(chip, k, chips) for k in range(chips)]
    peer = [2 * peer_chip[k] + core for k in range(chips)]
    barrier = pltpu.get_barrier_semaphore()
    pl.semaphore_signal(barrier, inc=1, device_id={"expert": pair}, device_id_type=MESH)
    for k in range(1, chips):
        pl.semaphore_signal(barrier, inc=1, device_id={"expert": peer[k]}, device_id_type=MESH)
    pl.semaphore_wait(barrier, chips)

    def remote(src, dst, send, recv, target):
        return pltpu.make_async_remote_copy(
            src_ref=src, dst_ref=dst, send_sem=send, recv_sem=recv,
            device_id={"expert": target}, device_id_type=MESH,
        )

    dispatch = {}
    for k in range(chips - 1, 0, -1):
        dispatch[k] = remote(packed.at[peer_chip[k]], got_a.at[k], send_a.at[k], recv_a.at[k], peer[k])
        dispatch[k].start()
    across, over, back = {}, {}, {}
    across[0] = remote(packed.at[chip], got_b.at[0], send_b.at[0], recv_b.at[0], pair)
    across[0].start()

    w_ready = False
    for group in groups_of:
        for k in group:
            if k:
                dispatch[k].wait_recv()
                across[k] = remote(got_a.at[k], got_b.at[k], send_b.at[k], recv_b.at[k], pair)
                across[k].start()
        for k in group:
            across[k].wait_recv()
            mine = got_a[k] if k else packed[chip]
            rows = jnp.concatenate([unfold(mine), unfold(got_b[k])], axis=0)
            x_ref[pl.ds(2 * cap * k, 2 * cap), :] = rows.astype(jnp.bfloat16)
        if not w_ready:
            load_1.wait()
            load_2.wait()
            w_ready = True
        first, count = 2 * cap * group[0], 2 * cap * len(group)
        block = pl.ds(first, count)
        hidden = h_scr.shape[1]
        width = part.shape[1]

        def hidden_tile(j, carry):
            columns = pl.ds(pl.multiple_of(j * TILE, TILE), TILE)
            if backward:
                value = lax.dot_general(
                    x_ref[block, :], w2[columns, :], NT, preferred_element_type=jnp.float32
                )
                mask = kept[block, columns].astype(jnp.float32) > 0
                h_scr[block, columns] = jnp.where(mask, value, 0.0).astype(jnp.bfloat16)
            else:
                value = jnp.dot(
                    x_ref[block, :], w1[:, columns], preferred_element_type=jnp.float32
                )
                value = jnp.maximum(value, 0.0).astype(jnp.bfloat16)
                h_scr[block, columns] = value
                kept[block, columns] = value
            return carry

        lax.fori_loop(0, hidden // TILE, hidden_tile, 0)

        def out_tile(j, carry):
            columns = pl.ds(pl.multiple_of(j * TILE, TILE), TILE)
            if backward:
                part[block, columns] = lax.dot_general(
                    h_scr[block, :], w1[columns, :], NT, preferred_element_type=jnp.float32
                )
            else:
                part[block, columns] = jnp.dot(
                    h_scr[block, :], w2[:, columns], preferred_element_type=jnp.float32
                )
            return carry

        lax.fori_loop(0, width // TILE, out_tile, 0)
        for k in group:
            theirs = part[pl.ds(2 * cap * k + cap, cap), :]
            to_pair[k] = fold(theirs).astype(jnp.bfloat16)
            over[k] = remote(to_pair.at[k], from_pair.at[k], send_c.at[k], recv_c.at[k], pair)
            over[k].start()
        for k in reversed(group):
            over[k].wait_recv()
            total = fold(part[pl.ds(2 * cap * k, cap), :]) + from_pair[k].astype(jnp.float32)
            if k:
                to_back[k] = total.astype(jnp.bfloat16)
                back[k] = remote(to_back.at[k], out.at[chip], send_d.at[k], recv_d.at[k], peer[k])
                back[k].start()
            else:
                out[chip] = total.astype(jnp.bfloat16)
    for k in range(chips):
        if k:
            dispatch[k].wait_send()
            back[k].wait_send()
            back[k].wait_recv()
        across[k].wait_send()
        over[k].wait_send()


def run_experts(packed, expert_in, expert_out, kept=None):
    chips, rows2, half = packed.shape
    backward = kept is not None
    rows = chips * rows2
    width, hidden = expert_in.shape[1:]
    groups_of = [list(range(chips // 2)), list(range(chips // 2, chips))]
    vmem = pl.BlockSpec(memory_space=pltpu.VMEM)
    hbm = pl.BlockSpec(memory_space=pl.ANY)
    message = jax.ShapeDtypeStruct(packed.shape, jnp.bfloat16)
    kept_shape = jax.ShapeDtypeStruct((rows, hidden), jnp.bfloat16)
    block = pltpu.VMEM(packed.shape, jnp.bfloat16)
    sems = pltpu.SemaphoreType.DMA((chips,))
    return pl.pallas_call(
        functools.partial(expert_kernel, chips, backward, groups_of),
        out_shape=message if backward else (message, kept_shape),
        in_specs=[vmem, hbm, hbm] + ([vmem] if backward else []),
        out_specs=vmem if backward else (vmem, vmem),
        scratch_shapes=[
            pltpu.VMEM((width, hidden), jnp.bfloat16),
            pltpu.VMEM((hidden, width), jnp.bfloat16),
            block,
            block,
            pltpu.VMEM((rows, width), jnp.bfloat16),
            pltpu.VMEM((rows, hidden), jnp.bfloat16),
            pltpu.VMEM((rows, width), jnp.float32),
            block,
            block,
            block,
            pltpu.SemaphoreType.DMA((2,)),
        ]
        + [sems] * 8,
        compiler_params=pltpu.CompilerParams(
            collective_id=1 if backward else 0,
            has_side_effects=True,
            vmem_limit_bytes=44 * 1024 * 1024,
        ),
        cost_estimate=pl.CostEstimate(
            flops=4 * rows * width * hidden, bytes_accessed=20 * 2**20, transcendentals=0
        ),
        name="experts_back" if backward else "experts",
    )(*((packed, expert_in, expert_out) + ((kept,) if backward else ())))


def slot_places(block_routes, experts, capacity):
    flat_ids = block_routes.reshape(-1)
    onehot = (flat_ids[:, None] == jnp.arange(experts, dtype=jnp.int32)[None, :]).astype(jnp.int32)
    earlier = jnp.cumsum(onehot, axis=0, dtype=jnp.int32) - onehot
    position = jnp.sum(earlier * onehot, axis=1, dtype=jnp.int32)
    return flat_ids * capacity + position


def body(
    tokens,
    segments,
    lengths,
    attn_gain,
    attn_weight,
    ffn_gain,
    routes,
    route_gates,
    expert_in,
    expert_out,
    teacher,
):
    devices = lax.axis_size("expert")
    experts = devices // SPLIT
    tok_count, model_width = tokens.shape
    row_count, length = segments.shape
    seg_count = teacher.shape[1]
    capacity = max(2, 5 * tok_count // (2 * experts))
    capacity = -(-capacity // 8) * 8
    allowed = key_allowed(segments, lengths)
    inputs = tokens.astype(jnp.float32).reshape(row_count, length, model_width)
    whole_weight = lax.all_gather(attn_weight, "expert", axis=1, tiled=True)
    hidden_state = attend(inputs, whole_weight, allowed, attn_gain, HEADS)
    hidden_flat = hidden_state.reshape(tok_count, model_width)

    def ffn_norm(source):
        return layer_norm(source, ffn_gain)

    normed_ffn, norm_pull = jax.vjp(ffn_norm, hidden_flat)
    normed_bf = normed_ffn.astype(jnp.bfloat16)
    slot_place = slot_places(routes, experts, capacity)
    slot_ids = jnp.arange(experts * capacity, dtype=jnp.int32)
    places = slot_place.reshape(tok_count, 2)
    chosen = [
        (slot_ids[:, None] == places[None, :, choice]).astype(jnp.bfloat16) for choice in range(2)
    ]

    def fold_rows(packed):
        shaped = packed.astype(jnp.bfloat16).reshape(experts, capacity, 2, model_width // 2)
        return jnp.swapaxes(shaped, 1, 2).reshape(experts, 2 * capacity, model_width // 2)

    def unfold_rows(returned):
        shaped = returned.reshape(experts, 2, capacity, model_width // 2)
        return jnp.swapaxes(shaped, 1, 2).reshape(experts * capacity, model_width)

    def pick(rows, choice):
        return lax.dot_general(
            chosen[choice], rows, (((0,), (0,)), ((), ())), preferred_element_type=jnp.float32
        )

    packed = jnp.dot(chosen[0] + chosen[1], normed_bf, preferred_element_type=jnp.float32)
    returned, activated = run_experts(fold_rows(packed), expert_in, expert_out)
    returned = unfold_rows(returned)
    expert_sum = (
        pick(returned, 0) * route_gates[:, 0:1] + pick(returned, 1) * route_gates[:, 1:2]
    )
    outputs = hidden_flat + expert_sum
    positions = jnp.arange(length, dtype=jnp.int32)
    live_mask = positions[None, :] < lengths[:, None]
    member_int = jnp.logical_and(
        segments[:, :, None] == jnp.arange(seg_count, dtype=jnp.int32)[None, None, :],
        live_mask[:, :, None],
    ).astype(jnp.int32)
    member = member_int.astype(jnp.float32)
    counts = jnp.sum(member_int, axis=1, dtype=jnp.int32)
    pooled = jnp.einsum(
        "rls,rld->rsd",
        member,
        outputs.reshape(row_count, length, model_width),
        precision=lax.Precision.HIGHEST,
    )
    pooled = pooled / jnp.maximum(counts, 1).astype(jnp.float32)[:, :, None]
    difference = pooled - teacher
    grad_out = jnp.einsum(
        "rls,rsd->rld", member, difference, precision=lax.Precision.HIGHEST
    ).reshape(tok_count, model_width)
    slot_grads = jnp.concatenate(
        [
            (grad_out * route_gates[:, choice : choice + 1]).astype(jnp.bfloat16)
            for choice in range(2)
        ],
        axis=0,
    )
    grad_packed = jnp.dot(
        jnp.concatenate(chosen, axis=1), slot_grads, preferred_element_type=jnp.float32
    )
    grad_back = run_experts(fold_rows(grad_packed), expert_in, expert_out, activated)
    grad_normed = lax.dot_general(
        chosen[0] + chosen[1],
        unfold_rows(grad_back),
        (((0,), (0,)), ((), ())),
        preferred_element_type=jnp.float32,
    )
    grad_hidden = (grad_out + norm_pull(grad_normed)[0]).reshape(row_count, length, model_width)
    again_weight = lax.all_gather(attn_weight, "expert", axis=1, tiled=True)

    def attention_again(source):
        return attend(source, again_weight, allowed, attn_gain, HEADS)

    grad_inputs = jax.vjp(attention_again, inputs)[1](grad_hidden)[0]
    grad_tokens = grad_inputs.reshape(tok_count, model_width).astype(jnp.bfloat16)
    return (grad_tokens, pooled)


def solution(mesh):
    placed = (
        P(("groups", "expert"), None),
        P(("groups", "expert"), None),
        P(("groups", "expert")),
        P(),
        P(None, "expert"),
        P(),
        P(("groups", "expert"), None),
        P(("groups", "expert"), None),
        P("expert", None, None),
        P("expert", None, None),
        P(("groups", "expert"), None, None),
    )
    return jax.shard_map(
        body,
        mesh=mesh,
        in_specs=placed,
        out_specs=(P(("groups", "expert"), None), P(("groups", "expert"), None, None)),
        check_vma=False,
    )
```

```python
import functools

import jax
import jax.numpy as jnp
from jax import lax
from jax.experimental import pallas as pl
from jax.experimental.pallas import tpu as pltpu
from jax.sharding import PartitionSpec as P

HEADS = 8
SPLIT = 2
MESH = pl.DeviceIdType.MESH
NT = (((1,), (1,)), ((), ()))
TILE = 256


epsilon = 1e-05


def layer_norm(inputs, scale_gain):
    average = jnp.mean(inputs, axis=-1, keepdims=True)
    centred = inputs - average
    variance = jnp.mean(centred * centred, axis=-1, keepdims=True)
    return centred * lax.rsqrt(variance + epsilon) * scale_gain


def key_allowed(segments, lengths):
    positions = jnp.arange(segments.shape[1], dtype=jnp.int32)
    same_seg = segments[:, :, None] == segments[:, None, :]
    key_live = positions[None, None, :] < lengths[:, None, None]
    itself = positions[:, None] == positions[None, :]
    return jnp.logical_or(jnp.logical_and(same_seg, key_live), itself[None])


def attend(inputs, weight, allowed, scale_gain, head_count):
    row_count, length, model_width = inputs.shape
    head_width = model_width // head_count
    normed = (
        layer_norm(inputs, scale_gain).astype(jnp.bfloat16).reshape(row_count * length, model_width)
    )
    projected = lax.dot_general(
        normed, weight[: 3 * model_width], NT, preferred_element_type=jnp.float32
    ).astype(jnp.bfloat16)
    projected = projected.reshape(row_count, length, 3, head_count, head_width)
    queries = projected[:, :, 0]
    keys_all = projected[:, :, 1]
    values_all = projected[:, :, 2]
    scores = jnp.einsum(
        "rqhd,rkhd->rhqk", queries, keys_all, preferred_element_type=jnp.float32
    ) * head_width ** (-0.5)
    weights_exp = jnp.exp(scores) * allowed[:, None].astype(jnp.float32)
    probabilities = (weights_exp / jnp.sum(weights_exp, axis=-1, keepdims=True)).astype(
        jnp.bfloat16
    )
    context = jnp.einsum(
        "rhqk,rkhd->rqhd", probabilities, values_all, preferred_element_type=jnp.float32
    ).astype(jnp.bfloat16)
    context = context.reshape(row_count * length, model_width)
    output = lax.dot_general(context, weight[3 * model_width :], NT, preferred_element_type=jnp.float32)
    return inputs + output.reshape(row_count, length, model_width)


def flip(index, bits, count):
    result, place = 0, 1
    while place < count:
        bit = lax.rem(lax.div(index, place), 2)
        if (bits // place) % 2:
            bit = 1 - bit
        result = result + bit * place
        place *= 2
    return result


def unfold(block):
    wide = block.astype(jnp.float32)
    cap = wide.shape[0] // 2
    return jnp.concatenate([wide[:cap], wide[cap:]], axis=1)


def fold(rows):
    half = rows.shape[1] // 2
    return jnp.concatenate([rows[:, :half], rows[:, half:]], axis=0)


def expert_kernel(chips, backward, groups_of, *refs):
    if backward:
        rows_in, w1_hbm, w2_hbm, kept, rows_out = refs[:5]
        rest = refs[5:]
    else:
        rows_in, w1_hbm, w2_hbm, rows_out, kept = refs[:5]
        rest = refs[5:]
    (packed, out, w1, w2, got_a, got_b, x_ref, h_scr, part, to_pair, from_pair, to_back,
     w_sem, send_a, recv_a, send_b, recv_b, send_c, recv_c, send_d, recv_d) = rest
    rank = lax.axis_index("expert")
    core = lax.rem(rank, 2)
    chip = lax.div(rank, 2)
    pair = 2 * chip + (1 - core)
    cap = packed.shape[1] // 2
    load_1 = pltpu.make_async_copy(w1_hbm.at[0], w1, w_sem.at[0])
    load_2 = pltpu.make_async_copy(w2_hbm.at[0], w2, w_sem.at[1])
    load_1.start()
    load_2.start()
    for e in range(chips):
        packed[e] = fold(rows_in[pl.ds(e * cap, cap), :]).astype(jnp.bfloat16)
    peer_chip = [flip(chip, k, chips) for k in range(chips)]
    peer = [2 * peer_chip[k] + core for k in range(chips)]
    barrier = pltpu.get_barrier_semaphore()
    pl.semaphore_signal(barrier, inc=1, device_id={"expert": pair}, device_id_type=MESH)
    for k in range(1, chips):
        pl.semaphore_signal(barrier, inc=1, device_id={"expert": peer[k]}, device_id_type=MESH)
    pl.semaphore_wait(barrier, chips)

    def remote(src, dst, send, recv, target):
        return pltpu.make_async_remote_copy(
            src_ref=src, dst_ref=dst, send_sem=send, recv_sem=recv,
            device_id={"expert": target}, device_id_type=MESH,
        )

    dispatch = {}
    for k in range(chips - 1, 0, -1):
        dispatch[k] = remote(packed.at[peer_chip[k]], got_a.at[k], send_a.at[k], recv_a.at[k], peer[k])
        dispatch[k].start()
    across, over, back = {}, {}, {}
    across[0] = remote(packed.at[chip], got_b.at[0], send_b.at[0], recv_b.at[0], pair)
    across[0].start()

    w_ready = False
    for group in groups_of:
        for k in group:
            if k:
                dispatch[k].wait_recv()
                across[k] = remote(got_a.at[k], got_b.at[k], send_b.at[k], recv_b.at[k], pair)
                across[k].start()
        for k in group:
            across[k].wait_recv()
            mine = got_a[k] if k else packed[chip]
            rows = jnp.concatenate([unfold(mine), unfold(got_b[k])], axis=0)
            x_ref[pl.ds(2 * cap * k, 2 * cap), :] = rows.astype(jnp.bfloat16)
        if not w_ready:
            load_1.wait()
            load_2.wait()
            w_ready = True
        first, count = 2 * cap * group[0], 2 * cap * len(group)
        block = pl.ds(first, count)
        hidden = h_scr.shape[1]
        width = part.shape[1]

        def hidden_tile(j, carry):
            columns = pl.ds(pl.multiple_of(j * TILE, TILE), TILE)
            if backward:
                value = lax.dot_general(
                    x_ref[block, :], w2[columns, :], NT, preferred_element_type=jnp.float32
                )
                mask = kept[block, columns].astype(jnp.float32) > 0
                h_scr[block, columns] = jnp.where(mask, value, 0.0).astype(jnp.bfloat16)
            else:
                value = jnp.dot(
                    x_ref[block, :], w1[:, columns], preferred_element_type=jnp.float32
                )
                value = jnp.maximum(value, 0.0).astype(jnp.bfloat16)
                h_scr[block, columns] = value
                kept[block, columns] = value
            return carry

        lax.fori_loop(0, hidden // TILE, hidden_tile, 0)

        def out_tile(j, carry):
            columns = pl.ds(pl.multiple_of(j * TILE, TILE), TILE)
            if backward:
                part[block, columns] = lax.dot_general(
                    h_scr[block, :], w1[columns, :], NT, preferred_element_type=jnp.float32
                )
            else:
                part[block, columns] = jnp.dot(
                    h_scr[block, :], w2[:, columns], preferred_element_type=jnp.float32
                )
            return carry

        lax.fori_loop(0, width // TILE, out_tile, 0)
        for k in group:
            theirs = part[pl.ds(2 * cap * k + cap, cap), :]
            to_pair[k] = fold(theirs).astype(jnp.bfloat16)
            over[k] = remote(to_pair.at[k], from_pair.at[k], send_c.at[k], recv_c.at[k], pair)
            over[k].start()
        for k in reversed(group):
            over[k].wait_recv()
            total = fold(part[pl.ds(2 * cap * k, cap), :]) + from_pair[k].astype(jnp.float32)
            if k:
                to_back[k] = total.astype(jnp.bfloat16)
                back[k] = remote(to_back.at[k], out.at[chip], send_d.at[k], recv_d.at[k], peer[k])
                back[k].start()
            else:
                out[chip] = total.astype(jnp.bfloat16)
    for k in range(chips):
        if k:
            dispatch[k].wait_send()
            back[k].wait_send()
            back[k].wait_recv()
        across[k].wait_send()
        over[k].wait_send()
    for e in range(chips):
        rows_out[pl.ds(e * cap, cap), :] = unfold(out[e])


def gather_kernel(devices, own, out, local_sem, send, recv):
    lines = devices // 4
    width = own.shape[1]
    half, quarter = width // 2, width // 4
    rank = lax.axis_index("expert")
    group = lax.axis_index("groups")
    core = lax.rem(rank, 2)
    side = lax.rem(lax.div(rank, 2), 2)
    line = lax.div(rank, 4)
    there = [flip(line, k, lines) for k in range(lines)]

    def name(k, x, c):
        return there[k] * 4 + x * 2 + c

    pair = {"expert": name(0, side, 1 - core)}
    x_peer = {"expert": name(0, 1 - side, core)}
    y_peer = {"groups": 1 - group, "expert": rank}
    z_peer = [{"expert": name(k, side, core)} for k in range(lines)]
    barrier = pltpu.get_barrier_semaphore()
    for target in [pair, x_peer, y_peer] + z_peer[1:]:
        pl.semaphore_signal(barrier, inc=1, device_id=target, device_id_type=MESH)
    pl.semaphore_wait(barrier, lines + 2)

    mine = (group * half, half)
    other = ((1 - group) * half, half)
    started = []

    def copy(kind, k, target, shard, columns, source=None):
        place = pl.ds(pl.multiple_of(columns[0], quarter), columns[1])
        dst = out.at[shard, :, place]
        src = dst if source is None else source.at[:, place]
        return pltpu.make_async_remote_copy(
            src_ref=src, dst_ref=dst, send_sem=send.at[kind, k], recv_sem=recv.at[kind, k],
            device_id=target, device_id_type=MESH,
        )

    def go(*args):
        made = copy(*args)
        made.start()
        started.append(made)

    ahead = side, core
    keep = pltpu.make_async_copy(own, out.at[rank], local_sem)
    keep.start()
    go(1, 0, x_peer, rank, mine, own)
    for k in range(1, lines):
        go(0, k, z_peer[k], rank, mine, own)
    go(4, 0, x_peer, rank, (other[0] + quarter, quarter), own)
    go(5, 0, pair, rank, (0, width), own)

    def landed(kind, k, shard, columns):
        copy(kind, k, pair, shard, columns).wait_recv()

    def first(k):
        shard = name(k, *ahead)
        landed(0, k, shard, mine)
        go(1, k, x_peer, shard, mine)
        go(2, k, y_peer, shard, mine)
        go(5, k, pair, shard, mine)

    def second(k):
        if k:
            shard = name(k, *ahead)
            landed(2, k, shard, other)
            go(4, k, x_peer, shard, (other[0] + quarter, quarter))
            go(7, k, pair, shard, other)
        shard = name(k, 1 - side, core)
        landed(1, k, shard, mine)
        go(3, k, y_peer, shard, (mine[0], quarter))
        go(6, k, pair, shard, mine)

    def third(k):
        shard = name(k, 1 - side, core)
        landed(4, k, shard, (other[0] + quarter, quarter))
        go(9, k, pair, shard, (other[0] + quarter, quarter))
        landed(3, k, shard, (other[0], quarter))
        go(8, k, pair, shard, (other[0], quarter))

    second(0)
    for k in range(1, lines):
        first(k)
        if k > 1:
            second(k - 1)
        third(k - 1)
    second(lines - 1)
    third(lines - 1)

    for k in range(lines):
        shard = name(k, side, 1 - core)
        across = name(k, 1 - side, 1 - core)
        if k:
            landed(5, k, shard, mine)
            landed(7, k, shard, other)
        else:
            landed(5, 0, shard, (0, width))
        landed(6, k, across, mine)
        landed(8, k, across, (other[0], quarter))
        landed(9, k, across, (other[0] + quarter, quarter))
    for made in started:
        made.wait_send()
    keep.wait()


def gather_weight(own, devices):
    lines = devices // 4
    gathered = pl.pallas_call(
        functools.partial(gather_kernel, devices),
        out_shape=jax.ShapeDtypeStruct((devices,) + own.shape, own.dtype),
        in_specs=[pl.BlockSpec(memory_space=pltpu.HBM)],
        out_specs=pl.BlockSpec(memory_space=pltpu.HBM),
        scratch_shapes=[
            pltpu.SemaphoreType.DMA,
            pltpu.SemaphoreType.DMA((10, lines)),
            pltpu.SemaphoreType.DMA((10, lines)),
        ],
        compiler_params=pltpu.CompilerParams(collective_id=2, has_side_effects=True),
        name="gather_weight",
    )(own)
    return gathered.reshape(devices * own.shape[0], own.shape[1])


def run_experts(rows_in, chips, expert_in, expert_out, kept=None):
    backward = kept is not None
    rows = 2 * rows_in.shape[0]
    width, hidden = expert_in.shape[1:]
    groups_of = [list(range(chips // 2)), list(range(chips // 2, chips))]
    vmem = pl.BlockSpec(memory_space=pltpu.VMEM)
    hbm = pl.BlockSpec(memory_space=pltpu.HBM)
    message = jax.ShapeDtypeStruct(rows_in.shape, jnp.float32)
    kept_shape = jax.ShapeDtypeStruct((rows, hidden), jnp.bfloat16)
    block = pltpu.VMEM((chips, rows // chips, width // 2), jnp.bfloat16)
    sems = pltpu.SemaphoreType.DMA((chips,))
    return pl.pallas_call(
        functools.partial(expert_kernel, chips, backward, groups_of),
        out_shape=message if backward else (message, kept_shape),
        in_specs=[vmem, hbm, hbm] + ([vmem] if backward else []),
        out_specs=vmem if backward else (vmem, vmem),
        scratch_shapes=[
            block,
            block,
            pltpu.VMEM((width, hidden), jnp.bfloat16),
            pltpu.VMEM((hidden, width), jnp.bfloat16),
            block,
            block,
            pltpu.VMEM((rows, width), jnp.bfloat16),
            pltpu.VMEM((rows, hidden), jnp.bfloat16),
            pltpu.VMEM((rows, width), jnp.float32),
            block,
            block,
            block,
            pltpu.SemaphoreType.DMA((2,)),
        ]
        + [sems] * 8,
        compiler_params=pltpu.CompilerParams(
            collective_id=1 if backward else 0,
            has_side_effects=True,
            vmem_limit_bytes=44 * 1024 * 1024,
        ),
        cost_estimate=pl.CostEstimate(
            flops=4 * rows * width * hidden, bytes_accessed=20 * 2**20, transcendentals=0
        ),
        name="experts_back" if backward else "experts",
    )(*((rows_in, expert_in, expert_out) + ((kept,) if backward else ())))


def slot_places(block_routes, experts, capacity):
    flat_ids = block_routes.reshape(-1)
    onehot = (flat_ids[:, None] == jnp.arange(experts, dtype=jnp.int32)[None, :]).astype(jnp.int32)
    earlier = jnp.cumsum(onehot, axis=0, dtype=jnp.int32) - onehot
    position = jnp.sum(earlier * onehot, axis=1, dtype=jnp.int32)
    return flat_ids * capacity + position


def body(
    tokens,
    segments,
    lengths,
    attn_gain,
    attn_weight,
    ffn_gain,
    routes,
    route_gates,
    expert_in,
    expert_out,
    teacher,
):
    devices = lax.axis_size("expert")
    experts = devices // SPLIT
    tok_count, model_width = tokens.shape
    row_count, length = segments.shape
    seg_count = teacher.shape[1]
    capacity = max(2, 5 * tok_count // (2 * experts))
    capacity = -(-capacity // 8) * 8
    allowed = key_allowed(segments, lengths)
    inputs = tokens.astype(jnp.float32).reshape(row_count, length, model_width)
    whole_weight = gather_weight(attn_weight.T, devices)
    hidden_state = attend(inputs, whole_weight, allowed, attn_gain, HEADS)
    hidden_flat = hidden_state.reshape(tok_count, model_width)

    def ffn_norm(source):
        return layer_norm(source, ffn_gain)

    normed_ffn, norm_pull = jax.vjp(ffn_norm, hidden_flat)
    normed_bf = normed_ffn.astype(jnp.bfloat16)
    slot_place = slot_places(routes, experts, capacity)
    slot_ids = jnp.arange(experts * capacity, dtype=jnp.int32)
    places = slot_place.reshape(tok_count, 2)
    chosen = [
        (slot_ids[:, None] == places[None, :, choice]).astype(jnp.bfloat16) for choice in range(2)
    ]

    def pick(rows, choice):
        return lax.dot_general(
            chosen[choice], rows, (((0,), (0,)), ((), ())), preferred_element_type=jnp.float32
        )

    packed = jnp.dot(chosen[0] + chosen[1], normed_bf, preferred_element_type=jnp.float32)
    returned, activated = run_experts(packed, experts, expert_in, expert_out)
    returned = returned.astype(jnp.bfloat16)
    expert_sum = (
        pick(returned, 0) * route_gates[:, 0:1] + pick(returned, 1) * route_gates[:, 1:2]
    )
    outputs = hidden_flat + expert_sum
    positions = jnp.arange(length, dtype=jnp.int32)
    live_mask = positions[None, :] < lengths[:, None]
    member_int = jnp.logical_and(
        segments[:, :, None] == jnp.arange(seg_count, dtype=jnp.int32)[None, None, :],
        live_mask[:, :, None],
    ).astype(jnp.int32)
    member = member_int.astype(jnp.float32)
    counts = jnp.sum(member_int, axis=1, dtype=jnp.int32)
    pooled = jnp.einsum(
        "rls,rld->rsd",
        member,
        outputs.reshape(row_count, length, model_width),
        precision=lax.Precision.HIGHEST,
    )
    pooled = pooled / jnp.maximum(counts, 1).astype(jnp.float32)[:, :, None]
    difference = pooled - teacher
    grad_out = jnp.einsum(
        "rls,rsd->rld", member, difference, precision=lax.Precision.HIGHEST
    ).reshape(tok_count, model_width)
    slot_grads = jnp.concatenate(
        [
            (grad_out * route_gates[:, choice : choice + 1]).astype(jnp.bfloat16)
            for choice in range(2)
        ],
        axis=0,
    )
    grad_packed = jnp.dot(
        jnp.concatenate(chosen, axis=1), slot_grads, preferred_element_type=jnp.float32
    )
    grad_back = run_experts(grad_packed, experts, expert_in, expert_out, activated)
    grad_normed = lax.dot_general(
        chosen[0] + chosen[1],
        grad_back.astype(jnp.bfloat16),
        (((0,), (0,)), ((), ())),
        preferred_element_type=jnp.float32,
    )
    grad_hidden = (grad_out + norm_pull(grad_normed)[0]).reshape(row_count, length, model_width)

    def attention_again(source):
        return attend(source, whole_weight, allowed, attn_gain, HEADS)

    grad_inputs = jax.vjp(attention_again, inputs)[1](grad_hidden)[0]
    grad_tokens = grad_inputs.reshape(tok_count, model_width).astype(jnp.bfloat16)
    return (grad_tokens, pooled)


def solution(mesh):
    placed = (
        P(("groups", "expert"), None),
        P(("groups", "expert"), None),
        P(("groups", "expert")),
        P(),
        P(None, "expert"),
        P(),
        P(("groups", "expert"), None),
        P(("groups", "expert"), None),
        P("expert", None, None),
        P("expert", None, None),
        P(("groups", "expert"), None, None),
    )
    return jax.shard_map(
        body,
        mesh=mesh,
        in_specs=placed,
        out_specs=(P(("groups", "expert"), None), P(("groups", "expert"), None, None)),
        check_vma=False,
    )
```

```python
import functools

import jax
import jax.numpy as jnp
from jax import lax
from jax.experimental import pallas as pl
from jax.experimental.pallas import tpu as pltpu
from jax.sharding import PartitionSpec as P

HEADS = 8
SPLIT = 2
MESH = pl.DeviceIdType.MESH
NT = (((1,), (1,)), ((), ()))
TILE = 256


epsilon = 1e-05


def layer_norm(inputs, scale_gain):
    average = jnp.mean(inputs, axis=-1, keepdims=True)
    centred = inputs - average
    variance = jnp.mean(centred * centred, axis=-1, keepdims=True)
    return centred * lax.rsqrt(variance + epsilon) * scale_gain


def key_allowed(segments, lengths):
    positions = jnp.arange(segments.shape[1], dtype=jnp.int32)
    same_seg = segments[:, :, None] == segments[:, None, :]
    key_live = positions[None, None, :] < lengths[:, None, None]
    itself = positions[:, None] == positions[None, :]
    return jnp.logical_or(jnp.logical_and(same_seg, key_live), itself[None])


def attend(inputs, weight, allowed, scale_gain, head_count):
    row_count, length, model_width = inputs.shape
    head_width = model_width // head_count
    normed = (
        layer_norm(inputs, scale_gain).astype(jnp.bfloat16).reshape(row_count * length, model_width)
    )
    projected = lax.dot_general(
        normed, weight, NT, preferred_element_type=jnp.float32
    ).astype(jnp.bfloat16)[:, : 3 * model_width]
    projected = projected.reshape(row_count, length, 3, head_count, head_width)
    queries = projected[:, :, 0]
    keys_all = projected[:, :, 1]
    values_all = projected[:, :, 2]
    scores = jnp.einsum(
        "rqhd,rkhd->rhqk", queries, keys_all, preferred_element_type=jnp.float32
    ) * head_width ** (-0.5)
    weights_exp = jnp.exp(scores) * allowed[:, None].astype(jnp.float32)
    probabilities = (weights_exp / jnp.sum(weights_exp, axis=-1, keepdims=True)).astype(
        jnp.bfloat16
    )
    context = jnp.einsum(
        "rhqk,rkhd->rqhd", probabilities, values_all, preferred_element_type=jnp.float32
    ).astype(jnp.bfloat16)
    context = context.reshape(row_count * length, model_width)
    output = lax.dot_general(context, weight[3 * model_width :], NT, preferred_element_type=jnp.float32)
    return inputs + output.reshape(row_count, length, model_width)


def flip(index, bits, count):
    result, place = 0, 1
    while place < count:
        bit = lax.rem(lax.div(index, place), 2)
        if (bits // place) % 2:
            bit = 1 - bit
        result = result + bit * place
        place *= 2
    return result


def unfold(block):
    wide = block.astype(jnp.float32)
    cap = wide.shape[0] // 2
    return jnp.concatenate([wide[:cap], wide[cap:]], axis=1)


def fold(rows):
    half = rows.shape[1] // 2
    return jnp.concatenate([rows[:, :half], rows[:, half:]], axis=0)


def expert_kernel(chips, backward, groups_of, order, *refs):
    if backward:
        rows_in, w1_hbm, w2_hbm, kept, rows_out = refs[:5]
        rest = refs[5:]
    else:
        rows_in, w1_hbm, w2_hbm, rows_out, kept = refs[:5]
        rest = refs[5:]
    (packed, out, w1, w2, got_a, got_b, x_ref, h_scr, part, to_pair, from_pair, to_back,
     w_sem, send_a, recv_a, send_b, recv_b, send_c, recv_c, send_d, recv_d) = rest
    rank = lax.axis_index("expert")
    core = lax.rem(rank, 2)
    chip = lax.div(rank, 2)
    pair = 2 * chip + (1 - core)
    cap = packed.shape[1] // 2
    load_1 = pltpu.make_async_copy(w1_hbm.at[0], w1, w_sem.at[0])
    load_2 = pltpu.make_async_copy(w2_hbm.at[0], w2, w_sem.at[1])
    load_1.start()
    load_2.start()
    for e in range(chips):
        packed[e] = fold(rows_in[pl.ds(e * cap, cap), :]).astype(jnp.bfloat16)
    peer_chip = [flip(chip, k, chips) for k in range(chips)]
    peer = [2 * peer_chip[k] + core for k in range(chips)]
    barrier = pltpu.get_barrier_semaphore()
    pl.semaphore_signal(barrier, inc=1, device_id={"expert": pair}, device_id_type=MESH)
    for k in range(1, chips):
        pl.semaphore_signal(barrier, inc=1, device_id={"expert": peer[k]}, device_id_type=MESH)
    pl.semaphore_wait(barrier, chips)

    def remote(src, dst, send, recv, target):
        return pltpu.make_async_remote_copy(
            src_ref=src, dst_ref=dst, send_sem=send, recv_sem=recv,
            device_id={"expert": target}, device_id_type=MESH,
        )

    dispatch = {}
    for k in order:
        dispatch[k] = remote(packed.at[peer_chip[k]], got_a.at[k], send_a.at[k], recv_a.at[k], peer[k])
        dispatch[k].start()
    across, over, back = {}, {}, {}
    across[0] = remote(packed.at[chip], got_b.at[0], send_b.at[0], recv_b.at[0], pair)
    across[0].start()

    w_ready = False
    for group in groups_of:
        for k in group:
            if k:
                dispatch[k].wait_recv()
                across[k] = remote(got_a.at[k], got_b.at[k], send_b.at[k], recv_b.at[k], pair)
                across[k].start()
        for k in group:
            across[k].wait_recv()
            mine = got_a[k] if k else packed[chip]
            rows = jnp.concatenate([unfold(mine), unfold(got_b[k])], axis=0)
            x_ref[pl.ds(2 * cap * k, 2 * cap), :] = rows.astype(jnp.bfloat16)
        if not w_ready:
            load_1.wait()
            load_2.wait()
            w_ready = True
        first, count = 2 * cap * group[0], 2 * cap * len(group)
        block = pl.ds(first, count)
        hidden = h_scr.shape[1]
        width = part.shape[1]

        def hidden_tile(j, carry):
            columns = pl.ds(pl.multiple_of(j * TILE, TILE), TILE)
            if backward:
                value = lax.dot_general(
                    x_ref[block, :], w2[columns, :], NT, preferred_element_type=jnp.float32
                )
                mask = kept[block, columns].astype(jnp.float32) > 0
                h_scr[block, columns] = jnp.where(mask, value, 0.0).astype(jnp.bfloat16)
            else:
                value = jnp.dot(
                    x_ref[block, :], w1[:, columns], preferred_element_type=jnp.float32
                )
                value = jnp.maximum(value, 0.0).astype(jnp.bfloat16)
                h_scr[block, columns] = value
                kept[block, columns] = value
            return carry

        lax.fori_loop(0, hidden // TILE, hidden_tile, 0)

        def out_tile(j, carry):
            columns = pl.ds(pl.multiple_of(j * TILE, TILE), TILE)
            if backward:
                part[block, columns] = lax.dot_general(
                    h_scr[block, :], w1[columns, :], NT, preferred_element_type=jnp.float32
                )
            else:
                part[block, columns] = jnp.dot(
                    h_scr[block, :], w2[:, columns], preferred_element_type=jnp.float32
                )
            return carry

        lax.fori_loop(0, width // TILE, out_tile, 0)
        for k in group:
            theirs = part[pl.ds(2 * cap * k + cap, cap), :]
            to_pair[k] = fold(theirs).astype(jnp.bfloat16)
            over[k] = remote(to_pair.at[k], from_pair.at[k], send_c.at[k], recv_c.at[k], pair)
            over[k].start()
        for k in group:
            over[k].wait_recv()
            total = fold(part[pl.ds(2 * cap * k, cap), :]) + from_pair[k].astype(jnp.float32)
            if k:
                to_back[k] = total.astype(jnp.bfloat16)
                back[k] = remote(to_back.at[k], out.at[chip], send_d.at[k], recv_d.at[k], peer[k])
                back[k].start()
            else:
                out[chip] = total.astype(jnp.bfloat16)
    for k in range(chips):
        if k:
            dispatch[k].wait_send()
            back[k].wait_send()
            back[k].wait_recv()
        across[k].wait_send()
        over[k].wait_send()
    for e in range(chips):
        rows_out[pl.ds(e * cap, cap), :] = unfold(out[e])


def gather_kernel(devices, own, out, local_sem, send, recv):
    lines = devices // 4
    width = own.shape[1]
    half, quarter = width // 2, width // 4
    rank = lax.axis_index("expert")
    group = lax.axis_index("groups")
    core = lax.rem(rank, 2)
    side = lax.rem(lax.div(rank, 2), 2)
    line = lax.div(rank, 4)

    def name(shift, x, c):
        return (line + shift) * 4 + x * 2 + c

    pair = {"expert": name(0, side, 1 - core)}
    x_peer = {"expert": name(0, 1 - side, core)}
    y_peer = {"groups": 1 - group, "expert": rank}
    z_peer = {shift: {"expert": name(shift, side, core)} for shift in (-1, 1)}
    exists = {-1: line > 0, 1: line < lines - 1}
    barrier = pltpu.get_barrier_semaphore()
    around = [
        {"expert": lax.rem(line + turn, lines) * 4 + side * 2 + core} for turn in (1, lines - 1)
    ]
    for target in [pair, x_peer, y_peer] + around:
        pl.semaphore_signal(barrier, inc=1, device_id=target, device_id_type=MESH)
    pl.semaphore_wait(barrier, 5)

    mine = (group * half, half)
    other = ((1 - group) * half, half)
    ends = (other[0] + quarter, quarter)

    def slot(shift):
        return 0 if shift == 0 else 2 * abs(shift) - (1 if shift < 0 else 0)

    def copy(kind, shift, target, shard, columns, source=None):
        place = pl.ds(pl.multiple_of(columns[0], quarter), columns[1])
        dst = out.at[shard, :, place]
        src = dst if source is None else source.at[:, place]
        at = slot(shift)
        return pltpu.make_async_remote_copy(
            src_ref=src, dst_ref=dst, send_sem=send.at[kind, at], recv_sem=recv.at[kind, at],
            device_id=target, device_id_type=MESH,
        )

    def go(*args):
        copy(*args).start()

    def landed(kind, shift, shard, columns):
        copy(kind, shift, pair, shard, columns).wait_recv()

    def sent(kind, shift, columns):
        copy(kind, shift, pair, rank, columns).wait_send()

    def present(shift):
        return line + shift >= 0 if shift < 0 else line + shift < lines

    keep = pltpu.make_async_copy(own, out.at[rank], local_sem)
    keep.start()
    go(1, 0, x_peer, rank, mine, own)
    for step in (-1, 1):
        @pl.when(exists[step])
        def _(step=step):
            go(0, -step, z_peer[step], rank, mine, own)
    go(4, 0, x_peer, rank, ends, own)
    go(5, 0, pair, rank, (0, width), own)

    def first(shift):
        shard = name(shift, side, core)
        landed(0, shift, shard, mine)
        step = 1 if shift < 0 else -1
        if abs(shift) < lines - 1:
            @pl.when(exists[step])
            def _():
                go(0, shift - step, z_peer[step], shard, mine)
        go(1, shift, x_peer, shard, mine)
        go(2, shift, y_peer, shard, mine)
        go(5, shift, pair, shard, mine)

    def second(shift):
        if shift:
            shard = name(shift, side, core)
            landed(2, shift, shard, other)
            go(4, shift, x_peer, shard, ends)
            go(7, shift, pair, shard, other)
        shard = name(shift, 1 - side, core)
        landed(1, shift, shard, mine)
        go(3, shift, y_peer, shard, (mine[0], quarter))
        go(6, shift, pair, shard, mine)

    def third(shift):
        shard = name(shift, 1 - side, core)
        landed(4, shift, shard, ends)
        go(9, shift, pair, shard, ends)
        landed(3, shift, shard, (other[0], quarter))
        go(8, shift, pair, shard, (other[0], quarter))

    def last(shift):
        shard = name(shift, side, 1 - core)
        across = name(shift, 1 - side, 1 - core)
        if shift:
            landed(5, shift, shard, mine)
            landed(7, shift, shard, other)
            for kind in (2, 7):
                sent(kind, shift, mine)
            sent(5, shift, mine)
            step = 1 if shift < 0 else -1
            if abs(shift) < lines - 1:
                @pl.when(exists[step])
                def _():
                    sent(0, shift - step, mine)
        else:
            landed(5, 0, shard, (0, width))
            sent(5, 0, (0, width))
            for step in (-1, 1):
                @pl.when(exists[step])
                def _(step=step):
                    sent(0, -step, mine)
        landed(6, shift, across, mine)
        landed(8, shift, across, (other[0], quarter))
        landed(9, shift, across, ends)
        for kind in (1, 6):
            sent(kind, shift, mine)
        for kind in (3, 4, 8, 9):
            sent(kind, shift, ends)

    def both(stage, distance):
        if distance == 0:
            stage(0)
            return
        for shift in (-distance, distance):
            @pl.when(present(shift))
            def _(shift=shift):
                stage(shift)

    for distance in range(1, lines + 2):
        if distance < lines:
            both(first, distance)
        if distance - 1 < lines:
            both(second, distance - 1)
        if distance >= 2:
            both(third, distance - 2)
    for distance in range(lines):
        both(last, distance)
    keep.wait()


def gather_weight(own, devices):
    lines = devices // 4
    gathered = pl.pallas_call(
        functools.partial(gather_kernel, devices),
        out_shape=jax.ShapeDtypeStruct((devices,) + own.shape, own.dtype),
        in_specs=[pl.BlockSpec(memory_space=pltpu.HBM)],
        out_specs=pl.BlockSpec(memory_space=pltpu.HBM),
        scratch_shapes=[
            pltpu.SemaphoreType.DMA,
            pltpu.SemaphoreType.DMA((10, 2 * lines - 1)),
            pltpu.SemaphoreType.DMA((10, 2 * lines - 1)),
        ],
        compiler_params=pltpu.CompilerParams(collective_id=2, has_side_effects=True),
        name="gather_weight",
    )(own)
    return gathered.reshape(devices * own.shape[0], own.shape[1])


def run_experts(rows_in, chips, expert_in, expert_out, kept=None):
    backward = kept is not None
    rows = 2 * rows_in.shape[0]
    width, hidden = expert_in.shape[1:]
    part = chips // 4
    groups_of = [list(range(i * part, (i + 1) * part)) for i in (0, 2, 3, 1)]
    order = groups_of[1] + groups_of[2] + groups_of[3] + groups_of[0][1:]
    vmem = pl.BlockSpec(memory_space=pltpu.VMEM)
    hbm = pl.BlockSpec(memory_space=pltpu.HBM)
    message = jax.ShapeDtypeStruct(rows_in.shape, jnp.float32)
    kept_shape = jax.ShapeDtypeStruct((rows, hidden), jnp.bfloat16)
    block = pltpu.VMEM((chips, rows // chips, width // 2), jnp.bfloat16)
    sems = pltpu.SemaphoreType.DMA((chips,))
    return pl.pallas_call(
        functools.partial(expert_kernel, chips, backward, groups_of, order),
        out_shape=message if backward else (message, kept_shape),
        in_specs=[vmem, hbm, hbm] + ([vmem] if backward else []),
        out_specs=vmem if backward else (vmem, vmem),
        scratch_shapes=[
            block,
            block,
            pltpu.VMEM((width, hidden), jnp.bfloat16),
            pltpu.VMEM((hidden, width), jnp.bfloat16),
            block,
            block,
            pltpu.VMEM((rows, width), jnp.bfloat16),
            pltpu.VMEM((rows, hidden), jnp.bfloat16),
            pltpu.VMEM((rows, width), jnp.float32),
            block,
            block,
            block,
            pltpu.SemaphoreType.DMA((2,)),
        ]
        + [sems] * 8,
        compiler_params=pltpu.CompilerParams(
            collective_id=1 if backward else 0,
            has_side_effects=True,
            vmem_limit_bytes=44 * 1024 * 1024,
        ),
        cost_estimate=pl.CostEstimate(
            flops=4 * rows * width * hidden, bytes_accessed=20 * 2**20, transcendentals=0
        ),
        name="experts_back" if backward else "experts",
    )(*((rows_in, expert_in, expert_out) + ((kept,) if backward else ())))


def slot_places(block_routes, experts, capacity):
    flat_ids = block_routes.reshape(-1)
    onehot = (flat_ids[:, None] == jnp.arange(experts, dtype=jnp.int32)[None, :]).astype(jnp.int32)
    earlier = jnp.cumsum(onehot, axis=0, dtype=jnp.int32) - onehot
    position = jnp.sum(earlier * onehot, axis=1, dtype=jnp.int32)
    return flat_ids * capacity + position


def body(
    tokens,
    segments,
    lengths,
    attn_gain,
    attn_weight,
    ffn_gain,
    routes,
    route_gates,
    expert_in,
    expert_out,
    teacher,
):
    devices = lax.axis_size("expert")
    experts = devices // SPLIT
    tok_count, model_width = tokens.shape
    row_count, length = segments.shape
    seg_count = teacher.shape[1]
    capacity = max(2, 5 * tok_count // (2 * experts))
    capacity = -(-capacity // 8) * 8
    allowed = key_allowed(segments, lengths)
    inputs = tokens.astype(jnp.float32).reshape(row_count, length, model_width)
    whole_weight = gather_weight(attn_weight.T, devices)
    hidden_state = attend(inputs, whole_weight, allowed, attn_gain, HEADS)
    hidden_flat = hidden_state.reshape(tok_count, model_width)

    def ffn_norm(source):
        return layer_norm(source, ffn_gain)

    normed_ffn, norm_pull = jax.vjp(ffn_norm, hidden_flat)
    normed_bf = normed_ffn.astype(jnp.bfloat16)
    slot_place = slot_places(routes, experts, capacity)
    slot_ids = jnp.arange(experts * capacity, dtype=jnp.int32)
    places = slot_place.reshape(tok_count, 2)
    chosen = [
        (slot_ids[:, None] == places[None, :, choice]).astype(jnp.bfloat16) for choice in range(2)
    ]

    def pick(rows, choice):
        return lax.dot_general(
            chosen[choice], rows, (((0,), (0,)), ((), ())), preferred_element_type=jnp.float32
        )

    packed = jnp.dot(chosen[0] + chosen[1], normed_bf, preferred_element_type=jnp.float32)
    returned, activated = run_experts(packed, experts, expert_in, expert_out)
    returned = returned.astype(jnp.bfloat16)
    expert_sum = (
        pick(returned, 0) * route_gates[:, 0:1] + pick(returned, 1) * route_gates[:, 1:2]
    )
    outputs = hidden_flat + expert_sum
    positions = jnp.arange(length, dtype=jnp.int32)
    live_mask = positions[None, :] < lengths[:, None]
    member_int = jnp.logical_and(
        segments[:, :, None] == jnp.arange(seg_count, dtype=jnp.int32)[None, None, :],
        live_mask[:, :, None],
    ).astype(jnp.int32)
    member = member_int.astype(jnp.float32)
    counts = jnp.sum(member_int, axis=1, dtype=jnp.int32)
    pooled = jnp.einsum(
        "rls,rld->rsd",
        member,
        outputs.reshape(row_count, length, model_width),
        precision=lax.Precision.HIGHEST,
    )
    pooled = pooled / jnp.maximum(counts, 1).astype(jnp.float32)[:, :, None]
    difference = pooled - teacher
    grad_out = jnp.einsum(
        "rls,rsd->rld", member, difference, precision=lax.Precision.HIGHEST
    ).reshape(tok_count, model_width)
    slot_grads = jnp.concatenate(
        [
            (grad_out * route_gates[:, choice : choice + 1]).astype(jnp.bfloat16)
            for choice in range(2)
        ],
        axis=0,
    )
    grad_packed = jnp.dot(
        jnp.concatenate(chosen, axis=1), slot_grads, preferred_element_type=jnp.float32
    )
    grad_back = run_experts(grad_packed, experts, expert_in, expert_out, activated)
    grad_normed = lax.dot_general(
        chosen[0] + chosen[1],
        grad_back.astype(jnp.bfloat16),
        (((0,), (0,)), ((), ())),
        preferred_element_type=jnp.float32,
    )
    grad_hidden = (grad_out + norm_pull(grad_normed)[0]).reshape(row_count, length, model_width)

    def attention_again(source):
        return attend(source, whole_weight, allowed, attn_gain, HEADS)

    grad_inputs = jax.vjp(attention_again, inputs)[1](grad_hidden)[0]
    grad_tokens = grad_inputs.reshape(tok_count, model_width).astype(jnp.bfloat16)
    return (grad_tokens, pooled)


def solution(mesh):
    placed = (
        P(("groups", "expert"), None),
        P(("groups", "expert"), None),
        P(("groups", "expert")),
        P(),
        P(None, "expert"),
        P(),
        P(("groups", "expert"), None),
        P(("groups", "expert"), None),
        P("expert", None, None),
        P("expert", None, None),
        P(("groups", "expert"), None, None),
    )
    return jax.shard_map(
        body,
        mesh=mesh,
        in_specs=placed,
        out_specs=(P(("groups", "expert"), None), P(("groups", "expert"), None, None)),
        check_vma=False,
    )
```

```python
import functools

import jax
import jax.numpy as jnp
from jax import lax
from jax.experimental import pallas as pl
from jax.experimental.pallas import tpu as pltpu
from jax.sharding import PartitionSpec as P

HEADS = 8
SPLIT = 2
MESH = pl.DeviceIdType.MESH
NT = (((1,), (1,)), ((), ()))
TILE = 256


epsilon = 1e-05


def layer_norm(inputs, scale_gain):
    average = jnp.mean(inputs, axis=-1, keepdims=True)
    centred = inputs - average
    variance = jnp.mean(centred * centred, axis=-1, keepdims=True)
    return centred * lax.rsqrt(variance + epsilon) * scale_gain


def key_allowed(segments, lengths):
    positions = jnp.arange(segments.shape[1], dtype=jnp.int32)
    same_seg = segments[:, :, None] == segments[:, None, :]
    key_live = positions[None, None, :] < lengths[:, None, None]
    itself = positions[:, None] == positions[None, :]
    return jnp.logical_or(jnp.logical_and(same_seg, key_live), itself[None])


def attend(inputs, weight, allowed, scale_gain, head_count):
    row_count, length, model_width = inputs.shape
    head_width = model_width // head_count
    normed = (
        layer_norm(inputs, scale_gain).astype(jnp.bfloat16).reshape(row_count * length, model_width)
    )
    projected = lax.dot_general(
        normed, weight, NT, preferred_element_type=jnp.float32
    ).astype(jnp.bfloat16)[:, : 3 * model_width]
    projected = projected.reshape(row_count, length, 3, head_count, head_width)
    queries = projected[:, :, 0]
    keys_all = projected[:, :, 1]
    values_all = projected[:, :, 2]
    scores = jnp.einsum(
        "rqhd,rkhd->rhqk", queries, keys_all, preferred_element_type=jnp.float32
    ) * head_width ** (-0.5)
    weights_exp = jnp.exp(scores) * allowed[:, None].astype(jnp.float32)
    probabilities = (weights_exp / jnp.sum(weights_exp, axis=-1, keepdims=True)).astype(
        jnp.bfloat16
    )
    context = jnp.einsum(
        "rhqk,rkhd->rqhd", probabilities, values_all, preferred_element_type=jnp.float32
    ).astype(jnp.bfloat16)
    context = context.reshape(row_count * length, model_width)
    output = lax.dot_general(context, weight[3 * model_width :], NT, preferred_element_type=jnp.float32)
    return inputs + output.reshape(row_count, length, model_width)


def flip(index, bits, count):
    result, place = 0, 1
    while place < count:
        bit = lax.rem(lax.div(index, place), 2)
        if (bits // place) % 2:
            bit = 1 - bit
        result = result + bit * place
        place *= 2
    return result


def unfold(block):
    wide = block.astype(jnp.float32)
    cap = wide.shape[0] // 2
    return jnp.concatenate([wide[:cap], wide[cap:]], axis=1)


def fold(rows):
    half = rows.shape[1] // 2
    return jnp.concatenate([rows[:, :half], rows[:, half:]], axis=0)


def expert_kernel(chips, backward, groups_of, order, *refs):
    if backward:
        rows_in, w1_hbm, w2_hbm, kept, rows_out = refs[:5]
        rest = refs[5:]
    else:
        rows_in, w1_hbm, w2_hbm, rows_out, kept = refs[:5]
        rest = refs[5:]
    (packed, out, w1, w2, got_a, got_b, x_ref, h_scr, part, to_pair, from_pair, to_back,
     w_sem, send_a, recv_a, send_b, recv_b, send_c, recv_c, send_d, recv_d) = rest
    rank = lax.axis_index("expert")
    core = lax.rem(rank, 2)
    chip = lax.div(rank, 2)
    pair = 2 * chip + (1 - core)
    cap = packed.shape[1] // 2
    spot = {k: i for i, k in enumerate(sum(groups_of, []))}
    load_1 = pltpu.make_async_copy(w1_hbm.at[0], w1, w_sem.at[0])
    load_2 = pltpu.make_async_copy(w2_hbm.at[0], w2, w_sem.at[1])
    load_1.start()
    load_2.start()
    for e in range(chips):
        packed[e] = fold(rows_in[pl.ds(e * cap, cap), :]).astype(jnp.bfloat16)
    peer_chip = [flip(chip, k, chips) for k in range(chips)]
    peer = [2 * peer_chip[k] + core for k in range(chips)]
    barrier = pltpu.get_barrier_semaphore()
    pl.semaphore_signal(barrier, inc=1, device_id={"expert": pair}, device_id_type=MESH)
    for k in range(1, chips):
        pl.semaphore_signal(barrier, inc=1, device_id={"expert": peer[k]}, device_id_type=MESH)
    pl.semaphore_wait(barrier, chips)

    def remote(src, dst, send, recv, target):
        return pltpu.make_async_remote_copy(
            src_ref=src, dst_ref=dst, send_sem=send, recv_sem=recv,
            device_id={"expert": target}, device_id_type=MESH,
        )

    dispatch = {}
    for k in order:
        dispatch[k] = remote(packed.at[peer_chip[k]], got_a.at[k], send_a.at[k], recv_a.at[k], peer[k])
        dispatch[k].start()
    across, over, back = {}, {}, {}
    across[0] = remote(packed.at[chip], got_b.at[0], send_b.at[0], recv_b.at[0], pair)
    across[0].start()

    w_ready = False
    for group in groups_of:
        for k in group:
            if k:
                dispatch[k].wait_recv()
                across[k] = remote(got_a.at[k], got_b.at[k], send_b.at[k], recv_b.at[k], pair)
                across[k].start()
        for k in group:
            across[k].wait_recv()
            mine = got_a[k] if k else packed[chip]
            rows = jnp.concatenate([unfold(mine), unfold(got_b[k])], axis=0)
            x_ref[pl.ds(2 * cap * spot[k], 2 * cap), :] = rows.astype(jnp.bfloat16)
        if not w_ready:
            load_1.wait()
            load_2.wait()
            w_ready = True
        first, count = 2 * cap * spot[group[0]], 2 * cap * len(group)
        block = pl.ds(first, count)
        hidden = h_scr.shape[1]
        width = part.shape[1]

        def hidden_tile(j, carry):
            columns = pl.ds(pl.multiple_of(j * TILE, TILE), TILE)
            if backward:
                value = lax.dot_general(
                    x_ref[block, :], w2[columns, :], NT, preferred_element_type=jnp.float32
                )
                mask = kept[block, columns].astype(jnp.float32) > 0
                h_scr[block, columns] = jnp.where(mask, value, 0.0).astype(jnp.bfloat16)
            else:
                value = jnp.dot(
                    x_ref[block, :], w1[:, columns], preferred_element_type=jnp.float32
                )
                value = jnp.maximum(value, 0.0).astype(jnp.bfloat16)
                h_scr[block, columns] = value
                kept[block, columns] = value
            return carry

        lax.fori_loop(0, hidden // TILE, hidden_tile, 0)

        def out_tile(j, carry):
            columns = pl.ds(pl.multiple_of(j * TILE, TILE), TILE)
            if backward:
                part[block, columns] = lax.dot_general(
                    h_scr[block, :], w1[columns, :], NT, preferred_element_type=jnp.float32
                )
            else:
                part[block, columns] = jnp.dot(
                    h_scr[block, :], w2[:, columns], preferred_element_type=jnp.float32
                )
            return carry

        lax.fori_loop(0, width // TILE, out_tile, 0)
        for k in group:
            theirs = part[pl.ds(2 * cap * spot[k] + cap, cap), :]
            to_pair[k] = fold(theirs).astype(jnp.bfloat16)
            over[k] = remote(to_pair.at[k], from_pair.at[k], send_c.at[k], recv_c.at[k], pair)
            over[k].start()
        for k in group:
            over[k].wait_recv()
            total = fold(part[pl.ds(2 * cap * spot[k], cap), :]) + from_pair[k].astype(jnp.float32)
            if k:
                to_back[k] = total.astype(jnp.bfloat16)
                back[k] = remote(to_back.at[k], out.at[chip], send_d.at[k], recv_d.at[k], peer[k])
                back[k].start()
            else:
                out[chip] = total.astype(jnp.bfloat16)
    for k in range(chips):
        if k:
            dispatch[k].wait_send()
            back[k].wait_send()
            back[k].wait_recv()
        across[k].wait_send()
        over[k].wait_send()
    for e in range(chips):
        rows_out[pl.ds(e * cap, cap), :] = unfold(out[e])


def gather_kernel(devices, own, out, local_sem, send, recv):
    lines = devices // 4
    width = own.shape[1]
    half, quarter = width // 2, width // 4
    rank = lax.axis_index("expert")
    group = lax.axis_index("groups")
    core = lax.rem(rank, 2)
    side = lax.rem(lax.div(rank, 2), 2)
    line = lax.div(rank, 4)

    def name(shift, x, c):
        return (line + shift) * 4 + x * 2 + c

    pair = {"expert": name(0, side, 1 - core)}
    x_peer = {"expert": name(0, 1 - side, core)}
    y_peer = {"groups": 1 - group, "expert": rank}
    z_peer = {shift: {"expert": name(shift, side, core)} for shift in (-1, 1)}
    exists = {-1: line > 0, 1: line < lines - 1}
    barrier = pltpu.get_barrier_semaphore()
    around = [
        {"expert": lax.rem(line + turn, lines) * 4 + side * 2 + core} for turn in (1, lines - 1)
    ]
    for target in [pair, x_peer, y_peer] + around:
        pl.semaphore_signal(barrier, inc=1, device_id=target, device_id_type=MESH)
    pl.semaphore_wait(barrier, 5)

    mine = (group * half, half)
    other = ((1 - group) * half, half)
    ends = (other[0] + quarter, quarter)

    def slot(shift):
        return 0 if shift == 0 else 2 * abs(shift) - (1 if shift < 0 else 0)

    def copy(kind, shift, target, shard, columns, source=None):
        place = pl.ds(pl.multiple_of(columns[0], quarter), columns[1])
        dst = out.at[shard, :, place]
        src = dst if source is None else source.at[:, place]
        at = slot(shift)
        return pltpu.make_async_remote_copy(
            src_ref=src, dst_ref=dst, send_sem=send.at[kind, at], recv_sem=recv.at[kind, at],
            device_id=target, device_id_type=MESH,
        )

    def go(*args):
        copy(*args).start()

    def landed(kind, shift, shard, columns):
        copy(kind, shift, pair, shard, columns).wait_recv()

    def sent(kind, shift, columns):
        copy(kind, shift, pair, rank, columns).wait_send()

    def present(shift):
        return line + shift >= 0 if shift < 0 else line + shift < lines

    keep = pltpu.make_async_copy(own, out.at[rank], local_sem)
    keep.start()
    go(1, 0, x_peer, rank, mine, own)
    for step in (-1, 1):
        @pl.when(exists[step])
        def _(step=step):
            go(0, -step, z_peer[step], rank, mine, own)
    go(4, 0, x_peer, rank, ends, own)
    go(5, 0, pair, rank, (0, width), own)

    def first(shift):
        shard = name(shift, side, core)
        landed(0, shift, shard, mine)
        step = 1 if shift < 0 else -1
        if abs(shift) < lines - 1:
            @pl.when(exists[step])
            def _():
                go(0, shift - step, z_peer[step], shard, mine)
        go(1, shift, x_peer, shard, mine)
        go(2, shift, y_peer, shard, mine)
        go(5, shift, pair, shard, mine)

    def second(shift):
        if shift:
            shard = name(shift, side, core)
            landed(2, shift, shard, other)
            go(4, shift, x_peer, shard, ends)
            go(7, shift, pair, shard, other)
        shard = name(shift, 1 - side, core)
        landed(1, shift, shard, mine)
        go(3, shift, y_peer, shard, (mine[0], quarter))
        go(6, shift, pair, shard, mine)

    def third(shift):
        shard = name(shift, 1 - side, core)
        landed(4, shift, shard, ends)
        go(9, shift, pair, shard, ends)
        landed(3, shift, shard, (other[0], quarter))
        go(8, shift, pair, shard, (other[0], quarter))

    def last(shift):
        shard = name(shift, side, 1 - core)
        across = name(shift, 1 - side, 1 - core)
        if shift:
            landed(5, shift, shard, mine)
            landed(7, shift, shard, other)
            for kind in (2, 7):
                sent(kind, shift, mine)
            sent(5, shift, mine)
            step = 1 if shift < 0 else -1
            if abs(shift) < lines - 1:
                @pl.when(exists[step])
                def _():
                    sent(0, shift - step, mine)
        else:
            landed(5, 0, shard, (0, width))
            sent(5, 0, (0, width))
            for step in (-1, 1):
                @pl.when(exists[step])
                def _(step=step):
                    sent(0, -step, mine)
        landed(6, shift, across, mine)
        landed(8, shift, across, (other[0], quarter))
        landed(9, shift, across, ends)
        for kind in (1, 6):
            sent(kind, shift, mine)
        for kind in (3, 4, 8, 9):
            sent(kind, shift, ends)

    def both(stage, distance):
        if distance == 0:
            stage(0)
            return
        for shift in (-distance, distance):
            @pl.when(present(shift))
            def _(shift=shift):
                stage(shift)

    for distance in range(1, lines + 2):
        if distance < lines:
            both(first, distance)
        if distance - 1 < lines:
            both(second, distance - 1)
        if distance >= 2:
            both(third, distance - 2)
    for distance in range(lines):
        both(last, distance)
    keep.wait()


def gather_weight(own, devices):
    lines = devices // 4
    gathered = pl.pallas_call(
        functools.partial(gather_kernel, devices),
        out_shape=jax.ShapeDtypeStruct((devices,) + own.shape, own.dtype),
        in_specs=[pl.BlockSpec(memory_space=pltpu.HBM)],
        out_specs=pl.BlockSpec(memory_space=pltpu.HBM),
        scratch_shapes=[
            pltpu.SemaphoreType.DMA,
            pltpu.SemaphoreType.DMA((10, 2 * lines - 1)),
            pltpu.SemaphoreType.DMA((10, 2 * lines - 1)),
        ],
        compiler_params=pltpu.CompilerParams(collective_id=2, has_side_effects=True),
        name="gather_weight",
    )(own)
    return gathered.reshape(devices * own.shape[0], own.shape[1])


def run_experts(rows_in, chips, expert_in, expert_out, kept=None):
    backward = kept is not None
    rows = 2 * rows_in.shape[0]
    width, hidden = expert_in.shape[1:]
    part = chips // 4
    near, side, far, last = [list(range(i * part, (i + 1) * part)) for i in range(4)]
    groups_of = [near + far, last + side] if backward else [near, far, last, side]
    order = far + last + side + near[1:]
    vmem = pl.BlockSpec(memory_space=pltpu.VMEM)
    hbm = pl.BlockSpec(memory_space=pltpu.HBM)
    message = jax.ShapeDtypeStruct(rows_in.shape, jnp.float32)
    kept_shape = jax.ShapeDtypeStruct((rows, hidden), jnp.bfloat16)
    block = pltpu.VMEM((chips, rows // chips, width // 2), jnp.bfloat16)
    sems = pltpu.SemaphoreType.DMA((chips,))
    return pl.pallas_call(
        functools.partial(expert_kernel, chips, backward, groups_of, order),
        out_shape=message if backward else (message, kept_shape),
        in_specs=[vmem, hbm, hbm] + ([vmem] if backward else []),
        out_specs=vmem if backward else (vmem, vmem),
        scratch_shapes=[
            block,
            block,
            pltpu.VMEM((width, hidden), jnp.bfloat16),
            pltpu.VMEM((hidden, width), jnp.bfloat16),
            block,
            block,
            pltpu.VMEM((rows, width), jnp.bfloat16),
            pltpu.VMEM((rows, hidden), jnp.bfloat16),
            pltpu.VMEM((rows, width), jnp.float32),
            block,
            block,
            block,
            pltpu.SemaphoreType.DMA((2,)),
        ]
        + [sems] * 8,
        compiler_params=pltpu.CompilerParams(
            collective_id=1 if backward else 0,
            has_side_effects=True,
            vmem_limit_bytes=44 * 1024 * 1024,
        ),
        cost_estimate=pl.CostEstimate(
            flops=4 * rows * width * hidden, bytes_accessed=20 * 2**20, transcendentals=0
        ),
        name="experts_back" if backward else "experts",
    )(*((rows_in, expert_in, expert_out) + ((kept,) if backward else ())))


def slot_places(block_routes, experts, capacity):
    flat_ids = block_routes.reshape(-1)
    onehot = (flat_ids[:, None] == jnp.arange(experts, dtype=jnp.int32)[None, :]).astype(jnp.int32)
    earlier = jnp.cumsum(onehot, axis=0, dtype=jnp.int32) - onehot
    position = jnp.sum(earlier * onehot, axis=1, dtype=jnp.int32)
    return flat_ids * capacity + position


def body(
    tokens,
    segments,
    lengths,
    attn_gain,
    attn_weight,
    ffn_gain,
    routes,
    route_gates,
    expert_in,
    expert_out,
    teacher,
):
    devices = lax.axis_size("expert")
    experts = devices // SPLIT
    tok_count, model_width = tokens.shape
    row_count, length = segments.shape
    seg_count = teacher.shape[1]
    capacity = max(2, 5 * tok_count // (2 * experts))
    capacity = -(-capacity // 8) * 8
    allowed = key_allowed(segments, lengths)
    inputs = tokens.astype(jnp.float32).reshape(row_count, length, model_width)
    whole_weight = gather_weight(attn_weight.T, devices)
    hidden_state = attend(inputs, whole_weight, allowed, attn_gain, HEADS)
    hidden_flat = hidden_state.reshape(tok_count, model_width)

    def ffn_norm(source):
        return layer_norm(source, ffn_gain)

    normed_ffn, norm_pull = jax.vjp(ffn_norm, hidden_flat)
    normed_bf = normed_ffn.astype(jnp.bfloat16)
    slot_place = slot_places(routes, experts, capacity)
    slot_ids = jnp.arange(experts * capacity, dtype=jnp.int32)
    places = slot_place.reshape(tok_count, 2)
    chosen = [
        (slot_ids[:, None] == places[None, :, choice]).astype(jnp.bfloat16) for choice in range(2)
    ]

    def pick(rows, choice):
        return lax.dot_general(
            chosen[choice], rows, (((0,), (0,)), ((), ())), preferred_element_type=jnp.float32
        )

    packed = jnp.dot(chosen[0] + chosen[1], normed_bf, preferred_element_type=jnp.float32)
    returned, activated = run_experts(packed, experts, expert_in, expert_out)
    returned = returned.astype(jnp.bfloat16)
    expert_sum = (
        pick(returned, 0) * route_gates[:, 0:1] + pick(returned, 1) * route_gates[:, 1:2]
    )
    outputs = hidden_flat + expert_sum
    positions = jnp.arange(length, dtype=jnp.int32)
    live_mask = positions[None, :] < lengths[:, None]
    member_int = jnp.logical_and(
        segments[:, :, None] == jnp.arange(seg_count, dtype=jnp.int32)[None, None, :],
        live_mask[:, :, None],
    ).astype(jnp.int32)
    member = member_int.astype(jnp.float32)
    counts = jnp.sum(member_int, axis=1, dtype=jnp.int32)
    pooled = jnp.einsum(
        "rls,rld->rsd",
        member,
        outputs.reshape(row_count, length, model_width),
        precision=lax.Precision.HIGHEST,
    )
    pooled = pooled / jnp.maximum(counts, 1).astype(jnp.float32)[:, :, None]
    difference = pooled - teacher
    grad_out = jnp.einsum(
        "rls,rsd->rld", member, difference, precision=lax.Precision.HIGHEST
    ).reshape(tok_count, model_width)
    slot_grads = jnp.concatenate(
        [
            (grad_out * route_gates[:, choice : choice + 1]).astype(jnp.bfloat16)
            for choice in range(2)
        ],
        axis=0,
    )
    grad_packed = jnp.dot(
        jnp.concatenate(chosen, axis=1), slot_grads, preferred_element_type=jnp.float32
    )
    grad_back = run_experts(grad_packed, experts, expert_in, expert_out, activated)
    grad_normed = lax.dot_general(
        chosen[0] + chosen[1],
        grad_back.astype(jnp.bfloat16),
        (((0,), (0,)), ((), ())),
        preferred_element_type=jnp.float32,
    )
    grad_hidden = (grad_out + norm_pull(grad_normed)[0]).reshape(row_count, length, model_width)

    def attention_again(source):
        return attend(source, whole_weight, allowed, attn_gain, HEADS)

    grad_inputs = jax.vjp(attention_again, inputs)[1](grad_hidden)[0]
    grad_tokens = grad_inputs.reshape(tok_count, model_width).astype(jnp.bfloat16)
    return (grad_tokens, pooled)


def solution(mesh):
    placed = (
        P(("groups", "expert"), None),
        P(("groups", "expert"), None),
        P(("groups", "expert")),
        P(),
        P(None, "expert"),
        P(),
        P(("groups", "expert"), None),
        P(("groups", "expert"), None),
        P("expert", None, None),
        P("expert", None, None),
        P(("groups", "expert"), None, None),
    )
    return jax.shard_map(
        body,
        mesh=mesh,
        in_specs=placed,
        out_specs=(P(("groups", "expert"), None), P(("groups", "expert"), None, None)),
        check_vma=False,
    )
```
